256 devices in a mesh: row: 32 (over z, y_hi, core), col: 8 (over y_lo, x).
Axes of the slice: x: 4, y: 4 (y_hi: 2, y_lo: 2; y = y_hi * 2 + y_lo), z: 8, core: 2. Of those that a mesh axis runs over, the one named last changes fastest.
Arguments:
- images: float32 [16384, 1152], P(('row', 'col')), may hold values from -0.17677669 to 0.17677669
- texts: float32 [16384, 1152], P(('row', 'col')), may hold values from -0.17677669 to 0.17677669
- logit_scale: float32 [1], replicated, may hold values from 40 to 120
- logit_bias: float32 [1], replicated, may hold values from -8 to -4
Outputs:
- image_grad: float32 [16384, 1152], P(('row', 'col'))
- text_grad: float32 [16384, 1152], P(('row', 'col'))
The draws below stay inside these ranges and needn't reach their ends.
All inputs are finite; a program needn't handle non-finite values.
Results may differ from the reference program's by a relative error of at most 0.009.
Values may be sent and summed in bfloat16 or wider, within the bound.
No kernel may reach another device: no remote copies, remote signals or barrier semaphores. Data moves between devices by JAX's collectives and lax.ppermute only.
A program may use at most 64 MiB of HBM per device.

```python
import jax
import jax.numpy as jnp
from jax import lax

D = 1152
PAIR_DEV = 64
PAIRS = 16384
N_COL = 8


def steps_of(stream_key, shape, cuts, smallest, top_value):
    level, own = 1.0, jax.random.fold_in(stream_key, 6)
    for dim, blocks in cuts:
        draws = jnp.exp(jax.random.uniform(jax.random.fold_in(own, dim), (blocks,), jnp.float32, smallest / len(cuts), top_value / len(cuts)))
        level = level * jnp.repeat(draws, shape[dim] // blocks).reshape([-1 if axis == dim else 1 for axis in range(len(shape))])
    return level


def bell_draw(stream_key, extent, deviation, reach, cuts=(), kind=jnp.bfloat16):
    level = steps_of(stream_key, extent, cuts, -0.22, 0.18) if cuts else 1.0
    values = jax.random.normal(stream_key, extent, jnp.float32) * deviation * level
    return jnp.minimum(jnp.maximum(values, -reach), reach).astype(kind)


def setup_inputs(seed: int = 0) -> dict:
    key_list = jax.random.split(jax.random.key(seed), 5)
    images = bell_draw(key_list[0], (PAIRS, D), (D ** -0.5), 0.17677669, ((0, 256),), jnp.float32)
    texts = bell_draw(key_list[1], (PAIRS, D), (D ** -0.5), 0.17677669, ((0, 256),), jnp.float32)
    logit_scale = jnp.clip(jax.random.uniform(key_list[2], (1,), jnp.float32, 40.0, 120.0), 40.0, 120.0)
    logit_bias = jnp.clip(jax.random.uniform(key_list[3], (1,), jnp.float32, -8.0, -4.0), -8.0, -4.0)
    return {"images": images, "texts": texts, "logit_scale": logit_scale, "logit_bias": logit_bias}


def normalize(raw):
    inv = lax.rsqrt(lax.optimization_barrier(jnp.sum(raw * raw, axis=1, keepdims=True)) + 1e-06)
    return ((raw * inv).astype(jnp.bfloat16), inv)

def unnormalize(raw, inv, grad):
    return inv * grad - raw * (inv * inv * inv) * lax.optimization_barrier(jnp.sum(raw * grad, axis=1, keepdims=True))

def reference(images, texts, logit_scale, logit_bias):
    img_norm, img_inv = normalize(images)
    txt_norm, txt_inv = normalize(texts)
    total = images.shape[0]
    block = PAIR_DEV * N_COL
    count = total // block
    scale = logit_scale[0]
    bias = logit_bias[0]
    text_ids = jnp.arange(total, dtype=jnp.int32)

    def step(carry, inputs):
        rows_norm, start = inputs
        row_ids = start + jnp.arange(block, dtype=jnp.int32)
        logits = scale * jnp.dot(rows_norm, txt_norm.T, preferred_element_type=jnp.float32) + bias
        sign = jnp.where(row_ids[:, None] == text_ids[None, :], 1.0, -1.0).astype(jnp.float32)
        weights = (-sign * jax.nn.sigmoid(-sign * logits)).astype(jnp.bfloat16)
        img_dir = scale * jnp.dot(weights, txt_norm, preferred_element_type=jnp.float32)
        carry = carry + scale * lax.dot_general(weights, rows_norm, (((0,), (0,)), ((), ())), preferred_element_type=jnp.float32)
        return (carry, img_dir)
    starts = jnp.arange(count, dtype=jnp.int32) * block
    txt_dir, img_blocks = lax.scan(step, jnp.zeros((total, D), jnp.float32), (img_norm.reshape(count, block, D), starts))
    img_dir = img_blocks.reshape(total, D)
    return (unnormalize(images, img_inv, img_dir), unnormalize(texts, txt_inv, txt_dir))
```

```python
import jax
import jax.numpy as jnp
from jax import lax
from jax.sharding import Mesh, PartitionSpec as P

AXES = ("z", "yh", "c", "yl", "x")
PLANE = ("yh", "yl", "x")
BF16 = jnp.bfloat16
F32 = jnp.float32


def shifted(value, axis, by):
    length = lax.axis_size(axis)
    return lax.ppermute(value, axis, [(i, (i + by) % length) for i in range(length)])


def normalize(raw):
    inv = lax.rsqrt(jnp.sum(raw * raw, axis=1, keepdims=True) + 1e-06)
    return ((raw * inv).astype(BF16), inv)


def unnormalize(raw, inv, grad):
    return inv * grad - raw * (inv * inv * inv) * jnp.sum(raw * grad, axis=1, keepdims=True)


def ring_gather(own):
    half = own.shape[0] // 2
    up, down, blocks = (own, own, [own])
    for _ in range(3):
        up, down = (shifted(up, "z", 1), shifted(down, "z", -1))
        blocks += [up, down]
    return blocks + [shifted(up[:half], "z", 1), shifted(down[half:], "z", -1)]


def added(a, b):
    return (a.astype(F32) + b.astype(F32)).astype(BF16)


def ring_scatter(blocks):
    own, m1, p1, m2, p2, m3, p3, far = blocks
    half = own.shape[0] // 2
    up = shifted(far[:half], "z", -1)
    down = shifted(far[half:], "z", 1)
    up = jnp.concatenate([added(m3[:half], up), m3[half:]], axis=0)
    down = jnp.concatenate([p3[:half], added(p3[half:], down)], axis=0)
    up, down = (shifted(up, "z", -1), shifted(down, "z", 1))
    up, down = (shifted(added(m2, up), "z", -1), shifted(added(p2, down), "z", 1))
    up, down = (shifted(added(m1, up), "z", -1), shifted(added(p1, down), "z", 1))
    return own.astype(F32) + up.astype(F32) + down.astype(F32)


def body(images, texts, logit_scale, logit_bias):
    rows, width = images.shape
    plane = lax.axis_size(PLANE)
    scale = logit_scale[0]
    bias = logit_bias[0]
    img_norm, img_inv = normalize(images)
    txt_norm, txt_inv = normalize(texts)

    copies = jnp.broadcast_to(txt_norm[None], (plane, rows, width))
    txt = lax.all_to_all(copies, PLANE, 0, 0, tiled=True).reshape(plane * rows, width)
    mine = jnp.concatenate(ring_gather(img_norm), axis=0)
    theirs = shifted(mine, "c", 1)
    img = jnp.concatenate([mine, theirs], axis=0)

    logits = (
        scale
        * lax.dot_general(txt, img, (((1,), (1,)), ((), ())), preferred_element_type=F32)
        + bias
    )
    place = lax.axis_index(PLANE) * rows
    txt_at = lax.broadcasted_iota(jnp.int32, logits.shape, 0)
    img_at = lax.broadcasted_iota(jnp.int32, logits.shape, 1)
    sign = jnp.where((txt_at - place == img_at) & (img_at < rows), 1.0, -1.0).astype(F32)
    weights = (-sign * jax.nn.sigmoid(-sign * logits)).astype(BF16)

    d_img = (
        scale * lax.dot_general(weights, txt, (((0,), (0,)), ((), ())), preferred_element_type=F32)
    )
    d_txt = (scale * jnp.dot(weights, img, preferred_element_type=F32)).astype(BF16)

    near = mine.shape[0]
    d_mine = d_img[:near] + shifted(d_img[near:].astype(BF16), "c", 1).astype(F32)
    d_mine = d_mine.astype(BF16)
    parts = lax.all_to_all(d_txt.reshape(plane, rows, width), PLANE, 0, 0, tiled=True)
    img_dir = ring_scatter([d_mine[i * rows : (i + 1) * rows] for i in range(near // rows)])
    txt_dir = jnp.sum(parts.astype(F32), axis=0)
    return (unnormalize(images, img_inv, img_dir), unnormalize(texts, txt_inv, txt_dir))


def solution(mesh):
    fine = Mesh(mesh.devices.reshape(8, 2, 2, 2, 4), AXES)
    rows = P(AXES, None)
    return jax.shard_map(
        body,
        mesh=fine,
        in_specs=(rows, rows, P(), P()),
        out_specs=(rows, rows),
        check_vma=False,
    )
```

```python
import jax
import jax.numpy as jnp
from jax import lax
from jax.experimental import pallas as pl
from jax.experimental.pallas import tpu as pltpu
from jax.sharding import Mesh, PartitionSpec as P

AXES = ("z", "yh", "c", "yl", "x")
PLANE = ("yh", "c", "yl", "x")
BF16 = jnp.bfloat16
F32 = jnp.float32


VMEM = pl.BlockSpec(memory_space=pltpu.VMEM)


def plane_groups():
    at = lambda y, c, x: ((y // 2 * 2 + c) * 2 + y % 2) * 4 + x
    along_x = [[[at(y, c, x) for x in range(4)] for y in range(4)] for c in range(2)]
    along_y = [[[at(y, c, x) for y in range(4)] for x in range(4)] for c in range(2)]
    return (along_x[0] + along_y[1], along_y[0] + along_x[1])


FIRST, SECOND = plane_groups()


def exchanged(blocks, groups):
    return lax.all_to_all(blocks, PLANE, 0, 0, tiled=True, axis_index_groups=groups)


def shifted(value, axis, by):
    length = lax.axis_size(axis)
    return lax.ppermute(value, axis, [(i, (i + by) % length) for i in range(length)])


def normalize_kernel(img_ref, txt_ref, img_out, txt_out):
    def norm(raw):
        inv = lax.rsqrt(jnp.sum(raw * raw, axis=1, keepdims=True) + 1e-06)
        return (raw * inv).astype(BF16)

    txt = norm(txt_ref[...])
    for i in range(txt_out.shape[0]):
        txt_out[i] = txt
    img_out[...] = norm(img_ref[...])


def normalize(images, texts, copies):
    return pl.pallas_call(
        normalize_kernel,
        out_shape=(
            jax.ShapeDtypeStruct(images.shape, BF16),
            jax.ShapeDtypeStruct((copies, *texts.shape), BF16),
        ),
        in_specs=[VMEM, VMEM],
        out_specs=(VMEM, VMEM),
    )(images, texts)


def unnormalize(raw, grad):
    inv = lax.rsqrt(jnp.sum(raw * raw, axis=1, keepdims=True) + 1e-06)
    return inv * grad - raw * (inv * inv * inv) * jnp.sum(raw * grad, axis=1, keepdims=True)


def ring_gather(own):
    half = own.shape[0] // 2
    up, down, blocks = (own, own, [own])
    for _ in range(3):
        up, down = (shifted(up, "z", 1), shifted(down, "z", -1))
        blocks += [up, down]
    return blocks + [shifted(up[:half], "z", 1), shifted(down[half:], "z", -1)]


def added(a, b):
    return (a.astype(F32) + b.astype(F32)).astype(BF16)


def ring_scatter(blocks):
    own, m1, p1, m2, p2, m3, p3, far = blocks
    half = own.shape[0] // 2
    up = shifted(far[:half], "z", -1)
    down = shifted(far[half:], "z", 1)
    up = jnp.concatenate([added(m3[:half], up), m3[half:]], axis=0)
    down = jnp.concatenate([p3[:half], added(p3[half:], down)], axis=0)
    up, down = (shifted(up, "z", -1), shifted(down, "z", 1))
    up, down = (shifted(added(m2, up), "z", -1), shifted(added(p2, down), "z", 1))
    up, down = (shifted(added(m1, up), "z", -1), shifted(added(p1, down), "z", 1))
    return own.astype(F32) + up.astype(F32) + down.astype(F32)


def body(images, texts, logit_scale, logit_bias):
    rows, width = images.shape
    line = len(FIRST[0])
    scale = logit_scale[0]
    bias = logit_bias[0]
    img_norm, txt_copies = normalize(images, texts, line)

    txt = exchanged(txt_copies, FIRST).reshape(1, line * rows, width)
    txt = jnp.broadcast_to(txt, (line, line * rows, width))
    txt = exchanged(txt, SECOND).reshape(line * line * rows, width)
    mine = jnp.concatenate(ring_gather(img_norm), axis=0)
    theirs = shifted(mine, "c", 1)
    img = jnp.concatenate([mine, theirs], axis=0)

    logits = (
        scale
        * lax.dot_general(txt, img, (((1,), (1,)), ((), ())), preferred_element_type=F32)
        + bias
    )
    core, x = (lax.axis_index("c"), lax.axis_index("x"))
    y = lax.axis_index(("yh", "yl"))
    place = jnp.where(core == 0, y * line + x, x * line + y) * rows
    txt_at = lax.broadcasted_iota(jnp.int32, logits.shape, 0)
    img_at = lax.broadcasted_iota(jnp.int32, logits.shape, 1)
    sign = jnp.where((txt_at - place == img_at) & (img_at < rows), 1.0, -1.0).astype(F32)
    weights = (-sign * jax.nn.sigmoid(-sign * logits)).astype(BF16)

    d_img = (
        scale * lax.dot_general(weights, txt, (((0,), (0,)), ((), ())), preferred_element_type=F32)
    )
    d_txt = (scale * jnp.dot(weights, img, preferred_element_type=F32)).astype(BF16)

    near = mine.shape[0]
    d_mine = d_img[:near] + shifted(d_img[near:].astype(BF16), "c", 1).astype(F32)
    d_mine = d_mine.astype(BF16)
    parts = exchanged(d_txt.reshape(line, line * rows, width), SECOND)
    parts = jnp.sum(parts.astype(F32), axis=0).astype(BF16)
    parts = exchanged(parts.reshape(line, rows, width), FIRST)
    img_dir = ring_scatter([d_mine[i * rows : (i + 1) * rows] for i in range(near // rows)])
    txt_dir = jnp.sum(parts.astype(F32), axis=0)
    return (unnormalize(images, img_dir), unnormalize(texts, txt_dir))


def solution(mesh):
    fine = Mesh(mesh.devices.reshape(8, 2, 2, 2, 4), AXES)
    rows = P(AXES, None)
    return jax.shard_map(
        body,
        mesh=fine,
        in_specs=(rows, rows, P(), P()),
        out_specs=(rows, rows),
        check_vma=False,
    )
```

```python
import functools

import jax
import jax.numpy as jnp
from jax import lax
from jax.experimental import pallas as pl
from jax.experimental.pallas import tpu as pltpu
from jax.sharding import Mesh, PartitionSpec as P

AXES = ("z", "yh", "c", "yl", "x")
PLANE = ("yh", "c", "yl", "x")
BF16 = jnp.bfloat16
F32 = jnp.float32
VMEM = pl.BlockSpec(memory_space=pltpu.VMEM)
SMEM = pl.BlockSpec(memory_space=pltpu.SMEM)
ROWS_TILE = 256


def plane_groups():
    at = lambda y, c, x: ((y // 2 * 2 + c) * 2 + y % 2) * 4 + x
    along_x = [[[at(y, c, x) for x in range(4)] for y in range(4)] for c in range(2)]
    along_y = [[[at(y, c, x) for y in range(4)] for x in range(4)] for c in range(2)]
    return (along_x[0] + along_y[1], along_y[0] + along_x[1])


FIRST, SECOND = plane_groups()


def exchanged(blocks, groups):
    return lax.all_to_all(blocks, PLANE, 0, 0, tiled=True, axis_index_groups=groups)


def shifted(value, axis, by):
    length = lax.axis_size(axis)
    return lax.ppermute(value, axis, [(i, (i + by) % length) for i in range(length)])


def shaped(shape, dtype):
    return jax.ShapeDtypeStruct(shape, dtype)


def local(kernel, outs, *args, scalars=0, flops=0, out_specs=None):
    specs = [SMEM] * scalars + [VMEM] * (len(args) - scalars)
    many = isinstance(outs, list)
    return pl.pallas_call(
        kernel,
        out_shape=outs,
        in_specs=specs,
        out_specs=out_specs or ([VMEM] * len(outs) if many else VMEM),
        compiler_params=pltpu.CompilerParams(vmem_limit_bytes=40 * 2**20),
        cost_estimate=pl.CostEstimate(
            flops=flops,
            bytes_accessed=sum(a.size * a.dtype.itemsize for a in args),
            transcendentals=0,
        ),
    )(*args)


def matmul(a, b, contract):
    return lax.dot_general(a, b, (contract, ((), ())), preferred_element_type=F32)


def inverse(raw):
    return lax.rsqrt(jnp.sum(raw * raw, axis=1, keepdims=True) + 1e-06)


def normalize_kernel(raw_ref, out_ref):
    raw = raw_ref[...]
    norm = (raw * inverse(raw)).astype(BF16)
    for i in range(out_ref.shape[0]):
        out_ref[i] = norm


def repeat_kernel(block_ref, out_ref):
    for i in range(out_ref.shape[0]):
        out_ref[i] = block_ref[...]


def join_kernel(*refs):
    *blocks, out_ref = refs
    rows = blocks[0].shape[0]
    for i, block in enumerate(blocks):
        out_ref[i * rows : (i + 1) * rows, :] = block[...]


def pair_kernel(rows, scale_ref, bias_ref, place_ref, img_ref, txt_ref, w_ref, d_ref):
    scale, bias = (scale_ref[0], bias_ref[0])
    for at in range(0, img_ref.shape[0], ROWS_TILE):
        tile = pl.ds(at, ROWS_TILE)
        logits = scale * matmul(img_ref[tile, :], txt_ref[...], ((1,), (1,))) + bias
        if at < rows:
            img_at = at + lax.broadcasted_iota(jnp.int32, logits.shape, 0)
            txt_at = lax.broadcasted_iota(jnp.int32, logits.shape, 1) - place_ref[0]
            sign = jnp.where((img_at == txt_at) & (img_at < rows), 1.0, -1.0).astype(F32)
            weights = -sign / (1.0 + jnp.exp(sign * logits))
        else:
            weights = 1.0 / (1.0 + jnp.exp(-logits))
        weights = weights.astype(BF16)
        w_ref[tile, :] = weights
        d_ref[tile, :] = (scale * matmul(weights, txt_ref[...], ((1,), (0,)))).astype(d_ref.dtype)


def text_kernel(scale_ref, w_mine_ref, w_theirs_ref, mine_ref, theirs_ref, d_ref):
    scale = scale_ref[0]
    for i in range(d_ref.shape[0]):
        cols = pl.ds(i * d_ref.shape[1], d_ref.shape[1])
        total = matmul(w_mine_ref[:, cols], mine_ref[...], ((0,), (0,)))
        total += matmul(w_theirs_ref[:, cols], theirs_ref[...], ((0,), (0,)))
        d_ref[i] = (scale * total).astype(BF16)


def split_kernel(mine_ref, theirs_ref, *outs):
    rows = outs[0].shape[0]
    for i, out in enumerate(outs):
        tile = pl.ds(i * rows, rows)
        out[...] = (mine_ref[tile, :] + theirs_ref[tile, :].astype(F32)).astype(out.dtype)


def add_kernel(a_ref, b_ref, out_ref):
    out_ref[...] = (a_ref[...].astype(F32) + b_ref[...].astype(F32)).astype(BF16)


def sum_kernel(parts_ref, out_ref):
    total = parts_ref[0].astype(F32)
    for i in range(1, parts_ref.shape[0]):
        total += parts_ref[i].astype(F32)
    rows = out_ref.shape[1]
    for i in range(out_ref.shape[0]):
        out_ref[i] = total[i * rows : (i + 1) * rows].astype(BF16)


def unnormalize(raw, grad):
    inv = inverse(raw)
    return inv * grad - raw * (inv * inv * inv) * jnp.sum(raw * grad, axis=1, keepdims=True)


def image_end_kernel(raw_ref, own_ref, up_ref, down_ref, out_ref):
    grad = own_ref[...] + up_ref[...].astype(F32) + down_ref[...].astype(F32)
    out_ref[...] = unnormalize(raw_ref[...], grad)


def text_end_kernel(raw_ref, parts_ref, out_ref):
    grad = parts_ref[0].astype(F32)
    for i in range(1, parts_ref.shape[0]):
        grad += parts_ref[i].astype(F32)
    out_ref[...] = unnormalize(raw_ref[...], grad)


def added(a, b):
    return local(add_kernel, shaped(a.shape, BF16), a, b)


def body(images, texts, scale, bias):
    rows, width = images.shape
    line = len(FIRST[0])
    ring = lax.axis_size("z")
    near, all_txt = (ring * rows, line * line * rows)
    txt_copies = local(normalize_kernel, shaped((line, rows, width), BF16), texts)
    img_norm = local(normalize_kernel, shaped((1, rows, width), BF16), images).reshape(rows, width)

    lines = exchanged(txt_copies, FIRST)
    up, down = (shifted(img_norm, "z", 1), shifted(img_norm, "z", -1))
    blocks = [img_norm, up, down]
    lines, up, down = lax.optimization_barrier((lines, up, down))
    copies = local(
        repeat_kernel,
        shaped((line, line * rows, width), BF16),
        lines.reshape(line * rows, width),
    )
    txt = exchanged(copies, SECOND).reshape(all_txt, width)
    for _ in range(2):
        up, down = (shifted(up, "z", 1), shifted(down, "z", -1))
        blocks += [up, down]
    blocks.append(shifted(up, "z", 1))
    mine = local(join_kernel, shaped((near, width), BF16), *blocks)
    theirs = shifted(mine, "c", 1)

    core, x = (lax.axis_index("c"), lax.axis_index("x"))
    y = lax.axis_index(("yh", "yl"))
    place = (jnp.where(core == 0, y * line + x, x * line + y) * rows).reshape(1)
    flops = 4 * near * all_txt * width
    pair = lambda paired, images_of, kind: local(
        functools.partial(pair_kernel, paired),
        [shaped((near, all_txt), BF16), shaped((near, width), kind)],
        scale, bias, place, images_of, txt,
        scalars=3, flops=flops,
    )
    w_mine, d_mine = pair(rows, mine, F32)
    w_theirs, d_theirs = pair(0, theirs, BF16)
    back = shifted(d_theirs, "c", 1)
    d_txt = local(
        text_kernel,
        shaped((line, line * rows, width), BF16),
        scale, w_mine, w_theirs, mine, theirs,
        scalars=1, flops=flops,
    )

    parts = exchanged(d_txt, SECOND)
    kinds = [F32] + [BF16] * (ring - 1)
    own, m1, p1, m2, p2, m3, p3, far = local(
        split_kernel, [shaped((rows, width), kind) for kind in kinds], d_mine, back
    )
    up, down = (shifted(far, "z", -1), shifted(p3, "z", 1))
    up, down = (shifted(added(m3, up), "z", -1), shifted(added(p2, down), "z", 1))
    up = shifted(added(m2, up), "z", -1)
    sums = local(sum_kernel, shaped((line, rows, width), BF16), parts)
    sums, up, down = lax.optimization_barrier((sums, up, down))
    ends = exchanged(sums, FIRST)
    up, down = (shifted(added(m1, up), "z", -1), shifted(added(p1, down), "z", 1))

    whole = pl.BlockSpec((rows, width), lambda: (0, 0))
    img_out = local(
        image_end_kernel, shaped((rows, width), F32), images, own, up, down, out_specs=whole
    )
    txt_out = local(text_end_kernel, shaped((rows, width), F32), texts, ends, out_specs=whole)
    return (img_out, txt_out)


def solution(mesh):
    fine = Mesh(mesh.devices.reshape(8, 2, 2, 2, 4), AXES)
    rows = P(AXES, None)
    return jax.shard_map(
        body,
        mesh=fine,
        in_specs=(rows, rows, P(), P()),
        out_specs=(rows, rows),
        check_vma=False,
    )
```

```python
import functools

import jax
import jax.numpy as jnp
from jax import lax
from jax.experimental import pallas as pl
from jax.experimental.pallas import tpu as pltpu
from jax.sharding import Mesh, PartitionSpec as P

AXES = ("z", "yh", "c", "yl", "x")
PLANE = ("yh", "c", "yl", "x")
BF16 = jnp.bfloat16
F32 = jnp.float32
VMEM = pl.BlockSpec(memory_space=pltpu.VMEM)
ANY = pl.BlockSpec(memory_space=pl.ANY)
HBM = pl.BlockSpec(memory_space=pltpu.HBM)
SMEM = pl.BlockSpec(memory_space=pltpu.SMEM)
ROWS_TILE = 256


def plane_groups():
    at = lambda y, c, x: ((y // 2 * 2 + c) * 2 + y % 2) * 4 + x
    along_x = [[[at(y, c, x) for x in range(4)] for y in range(4)] for c in range(2)]
    along_y = [[[at(y, c, x) for y in range(4)] for x in range(4)] for c in range(2)]
    return (along_x[0] + along_y[1], along_y[0] + along_x[1])


FIRST, SECOND = plane_groups()


def exchanged(blocks, groups):
    return lax.all_to_all(blocks, PLANE, 0, 0, tiled=True, axis_index_groups=groups)


def shifted(value, axis, by):
    length = lax.axis_size(axis)
    return lax.ppermute(value, axis, [(i, (i + by) % length) for i in range(length)])


def shaped(shape, dtype):
    return jax.ShapeDtypeStruct(shape, dtype)


def local(kernel, outs, *args, ins=None, out_specs=None, scratch=(), flops=0, aliases=None):
    many = isinstance(outs, list)
    ins = ins or [VMEM] * len(args)
    out_specs = out_specs or ([VMEM] * len(outs) if many else VMEM)
    placed = lambda out, spec: pltpu.HBM(out.shape, out.dtype) if spec is HBM else out
    outs = list(map(placed, outs, out_specs)) if many else placed(outs, out_specs)
    args = [
        pltpu.with_memory_space_constraint(arg, pltpu.HBM) if spec is HBM else arg
        for arg, spec in zip(args, ins)
    ]
    return pl.pallas_call(
        kernel,
        out_shape=outs,
        in_specs=ins,
        out_specs=out_specs,
        scratch_shapes=list(scratch),
        input_output_aliases=aliases or {},
        compiler_params=pltpu.CompilerParams(vmem_limit_bytes=16 * 2**20),
        cost_estimate=pl.CostEstimate(
            flops=flops,
            bytes_accessed=sum(a.size * a.dtype.itemsize for a in args),
            transcendentals=0,
        ),
    )(*args)


def matmul(a, b, contract):
    return lax.dot_general(a, b, (contract, ((), ())), preferred_element_type=F32)


def inverse(raw):
    return lax.rsqrt(jnp.sum(raw * raw, axis=1, keepdims=True) + 1e-06)


def copied(copies):
    for copy in copies:
        copy.start()
    for copy in copies:
        copy.wait()


def normalize_kernel(img_in, txt_in, img_out, txt_out, raw, img_buf, txt_buf, sems):
    reads = [
        pltpu.make_async_copy(a, raw.at[i], sems.at[0, i]) for i, a in enumerate((img_in, txt_in))
    ]
    for read in reads:
        read.start()
    reads[1].wait()
    txt = raw[1]
    txt_buf[...] = (txt * inverse(txt)).astype(BF16)
    writes = [
        pltpu.make_async_copy(txt_buf, txt_out.at[i], sems.at[1, i])
        for i in range(txt_out.shape[0])
    ]
    for write in writes:
        write.start()
    reads[0].wait()
    img = raw[0]
    img_buf[...] = (img * inverse(img)).astype(BF16)
    writes.append(pltpu.make_async_copy(img_buf, img_out, sems.at[0, 2]))
    writes[-1].start()
    for write in writes:
        write.wait()


def repeat_kernel(block_ref, out_ref, sems):
    copied(
        [pltpu.make_async_copy(block_ref, out_ref.at[i], sems.at[i]) for i in range(out_ref.shape[0])]
    )


def join_kernel(first, *refs):
    *blocks, out_ref, sems = refs
    rows = out_ref.shape[0] // sems.shape[0]
    at = lambda i: out_ref.at[pl.ds((first + i) * rows, rows), :]
    blocks = blocks[1:] if first else blocks
    copied([pltpu.make_async_copy(block, at(i), sems.at[i]) for i, block in enumerate(blocks)])


def weights_of(img_ref, txt_ref, tile, scale, bias, paired=0, place=None):
    at, size = tile
    logits = scale * matmul(img_ref[pl.ds(at, size), :], txt_ref[...], ((1,), (1,))) + bias
    if at >= paired:
        return (1.0 / (1.0 + jnp.exp(-logits))).astype(BF16)
    img_at = at + lax.broadcasted_iota(jnp.int32, logits.shape, 0)
    txt_at = lax.broadcasted_iota(jnp.int32, logits.shape, 1) - place
    sign = jnp.where((img_at == txt_at) & (img_at < paired), 1.0, -1.0).astype(F32)
    return (-sign / (1.0 + jnp.exp(sign * logits))).astype(BF16)


def tiles(rows):
    return [(at, ROWS_TILE) for at in range(0, rows, ROWS_TILE)]


def leave(copies, buffer, out, tile, sems):
    part = (pl.ds(*tile), slice(None))
    copies.append(pltpu.make_async_copy(buffer.at[part], out.at[part], sems.at[len(copies)]))
    copies[-1].start()


def mine_kernel(
    paired, scale_ref, bias_ref, place_ref, img_ref, txt_ref, w_ref, d_out, d_buf, sems
):
    scale, copies = (scale_ref[0], [])
    for tile in tiles(img_ref.shape[0]):
        weights = weights_of(img_ref, txt_ref, tile, scale, bias_ref[0], paired, place_ref[0])
        w_ref[pl.ds(*tile), :] = weights
        d_buf[pl.ds(*tile), :] = scale * matmul(weights, txt_ref[...], ((1,), (0,)))
        leave(copies, d_buf, d_out, tile, sems)
    for copy in copies:
        copy.wait()


def theirs_kernel(scale_ref, bias_ref, _, img_ref, txt_ref, w_ref, d_ref):
    scale = scale_ref[0]
    for tile in tiles(img_ref.shape[0]):
        weights = weights_of(img_ref, txt_ref, tile, scale, bias_ref[0])
        w_ref[pl.ds(*tile), :] = weights
        d_ref[pl.ds(*tile), :] = (scale * matmul(weights, txt_ref[...], ((1,), (0,)))).astype(BF16)


def text_kernel(scale_ref, w_mine_ref, w_theirs_ref, mine_ref, theirs_ref, d_out, d_buf, sems):
    scale, copies = (scale_ref[0], [])
    for tile in tiles(d_buf.shape[0]):
        total = matmul(w_mine_ref[:, pl.ds(*tile)], mine_ref[...], ((0,), (0,)))
        total += matmul(w_theirs_ref[:, pl.ds(*tile)], theirs_ref[...], ((0,), (0,)))
        d_buf[pl.ds(*tile), :] = (scale * total).astype(BF16)
        leave(copies, d_buf, d_out, tile, sems)
    for copy in copies:
        copy.wait()


def split_kernel(late, mine_in, theirs_in, *refs):
    *outs, mine, theirs, own_buf, late_buf, sems = refs
    rows = outs[0].shape[0]
    arriving, leaving = ([], [])
    for i in reversed(range(len(outs))):
        tile = (pl.ds(i * rows, rows), slice(None))
        pair = [
            pltpu.make_async_copy(mine_in.at[tile], mine.at[tile], sems.at[0, i]),
            pltpu.make_async_copy(theirs_in.at[tile], theirs.at[tile], sems.at[1, i]),
        ]
        for copy in pair:
            copy.start()
        arriving.append((i, tile, pair))
    for i, tile, pair in arriving:
        for copy in pair:
            copy.wait()
        out = outs[i]
        buffer = out if i >= late else late_buf.at[i - 1] if i else own_buf
        buffer[...] = (mine[tile] + theirs[tile].astype(F32)).astype(out.dtype)
        if i < late:
            leaving.append(pltpu.make_async_copy(buffer, out, sems.at[2, i]))
            leaving[-1].start()
    for copy in leaving:
        copy.wait()


def add_kernel(a_ref, b_ref, out_ref):
    out_ref[...] = (a_ref[...].astype(F32) + b_ref[...].astype(F32)).astype(BF16)


def sum_kernel(parts_ref, out_ref, buffer, sem):
    total = parts_ref[0].astype(F32)
    for i in range(1, parts_ref.shape[0]):
        total += parts_ref[i].astype(F32)
    rows = out_ref.shape[1]
    for i in range(out_ref.shape[0]):
        buffer[i] = total[i * rows : (i + 1) * rows].astype(BF16)
    copied([pltpu.make_async_copy(buffer, out_ref, sem)])


def unnormalize(raw, grad):
    inv = inverse(raw)
    return inv * grad - raw * (inv * inv * inv) * jnp.sum(raw * grad, axis=1, keepdims=True)


def image_end_kernel(raw_ref, own_ref, up_ref, down_ref, out_ref):
    grad = own_ref[...] + up_ref[...].astype(F32) + down_ref[...].astype(F32)
    out_ref[...] = unnormalize(raw_ref[...], grad)


def text_end_kernel(raw_ref, parts_ref, out_ref):
    grad = parts_ref[0].astype(F32)
    for i in range(1, parts_ref.shape[0]):
        grad += parts_ref[i].astype(F32)
    out_ref[...] = unnormalize(raw_ref[...], grad)


def added(a, b):
    return local(add_kernel, shaped(a.shape, BF16), a, b)


def body(images, texts, scale, bias):
    rows, width = images.shape
    line, ring = (len(FIRST[0]), lax.axis_size("z"))
    near, all_txt = (ring * rows, line * line * rows)
    copies_of = lambda *shape: pltpu.SemaphoreType.DMA(shape)

    img_norm, txt_copies = local(
        normalize_kernel,
        [shaped((rows, width), BF16), shaped((line, rows, width), BF16)],
        images, texts,
        ins=[HBM, HBM],
        out_specs=[HBM, HBM],
        scratch=[pltpu.VMEM((2, rows, width), F32)]
        + [pltpu.VMEM((rows, width), BF16)] * 2
        + [copies_of(2, line)],
    )
    lines = exchanged(txt_copies, FIRST).reshape(line * rows, width)
    up, down = (shifted(img_norm, "z", 1), shifted(img_norm, "z", -1))
    blocks = [img_norm, up, down]
    lines, up, down = lax.optimization_barrier((lines, up, down))
    up, down = (shifted(up, "z", 1), shifted(down, "z", -1))
    blocks += [up, down]
    copies = local(
        repeat_kernel,
        shaped((line, line * rows, width), BF16),
        lines,
        ins=[ANY],
        out_specs=HBM,
        scratch=[copies_of(line)],
    )
    txt = exchanged(copies, SECOND).reshape(all_txt, width)
    up, down = (shifted(up, "z", 1), shifted(down, "z", -1))
    blocks += [up, down]
    join = lambda first, ins, *args: local(
        functools.partial(join_kernel, first),
        shaped((near, width), BF16),
        *args,
        ins=ins,
        scratch=[copies_of(ring)],
        aliases={0: 0} if first else {},
    )
    mine = join(0, [HBM] * 3 + [ANY] * 4, *blocks)
    far = shifted(up, "z", 1)
    mine = join(ring - 1, [VMEM, ANY], mine, far)
    theirs = shifted(mine, "c", 1)

    core, x = (lax.axis_index("c"), lax.axis_index("x"))
    y = lax.axis_index(("yh", "yl"))
    place = (jnp.where(core == 0, y * line + x, x * line + y) * rows).reshape(1)
    flops = 2 * near * all_txt * width
    w_shape = shaped((near, all_txt), BF16)
    w_mine, d_mine = local(
        functools.partial(mine_kernel, rows),
        [w_shape, shaped((near, width), F32)],
        scale, bias, place, mine, txt,
        ins=[SMEM] * 3 + [VMEM] * 2,
        out_specs=[VMEM, HBM],
        scratch=[pltpu.VMEM((near, width), F32), copies_of(near // ROWS_TILE)],
        flops=2 * flops,
    )
    w_theirs, d_theirs = local(
        theirs_kernel,
        [w_shape, shaped((near, width), BF16)],
        scale, bias, w_mine, theirs, txt,
        ins=[SMEM] * 2 + [ANY] + [VMEM] * 2,
        flops=2 * flops,
    )
    back = shifted(d_theirs, "c", 1)
    d_txt = local(
        text_kernel,
        shaped((all_txt, width), BF16),
        scale, w_mine, w_theirs, mine, theirs,
        ins=[SMEM] + [VMEM] * 4,
        out_specs=HBM,
        scratch=[pltpu.VMEM((all_txt, width), BF16), copies_of(all_txt // ROWS_TILE)],
        flops=2 * flops,
    )

    d_txt, back = lax.optimization_barrier((d_txt, back))
    parts = exchanged(d_txt.reshape(line, line * rows, width), SECOND)
    kinds = [F32] + [BF16] * (ring - 1)
    late = 3
    own, m1, p1, m2, p2, m3, p3, far = local(
        functools.partial(split_kernel, late),
        [shaped((rows, width), kind) for kind in kinds],
        d_mine, back,
        ins=[HBM, HBM],
        out_specs=[HBM] * late + [VMEM] * (ring - late),
        scratch=[
            pltpu.VMEM((near, width), F32),
            pltpu.VMEM((near, width), BF16),
            pltpu.VMEM((rows, width), F32),
            pltpu.VMEM((late - 1, rows, width), BF16),
            copies_of(3, ring),
        ],
    )
    up, down = (shifted(far, "z", -1), shifted(p3, "z", 1))
    up, down = (shifted(added(m3, up), "z", -1), shifted(added(p2, down), "z", 1))
    up = shifted(added(m2, up), "z", -1)
    sums = local(
        sum_kernel,
        shaped((line, rows, width), BF16),
        parts,
        out_specs=HBM,
        scratch=[pltpu.VMEM((line, rows, width), BF16), copies_of()],
    )
    sums, up, down = lax.optimization_barrier((sums, up, down))
    ends = exchanged(sums, FIRST)
    up, down = (shifted(added(m1, up), "z", -1), shifted(added(p1, down), "z", 1))

    whole = pl.BlockSpec((rows, width), lambda: (0, 0))
    img_out = local(
        image_end_kernel, shaped((rows, width), F32), images, own, up, down, out_specs=whole
    )
    txt_out = local(text_end_kernel, shaped((rows, width), F32), texts, ends, out_specs=whole)
    return (img_out, txt_out)


def solution(mesh):
    fine = Mesh(mesh.devices.reshape(8, 2, 2, 2, 4), AXES)
    rows = P(AXES, None)
    return jax.shard_map(
        body,
        mesh=fine,
        in_specs=(rows, rows, P(), P()),
        out_specs=(rows, rows),
        check_vma=False,
    )
```

```python
import functools

import jax
import jax.numpy as jnp
from jax import lax
from jax.experimental import pallas as pl
from jax.experimental.pallas import tpu as pltpu
from jax.sharding import Mesh, PartitionSpec as P

AXES = ("z", "yh", "c", "yl", "x")
PLANE = ("yh", "c", "yl", "x")
SIDE = 4
BF16 = jnp.bfloat16
F32 = jnp.float32
VMEM = pl.BlockSpec(memory_space=pltpu.VMEM)
SMEM = pl.BlockSpec(memory_space=pltpu.SMEM)
TILE = 256


def shifted(value, axis, by):
    length = lax.axis_size(axis)
    return lax.ppermute(value, axis, [(i, (i + by) % length) for i in range(length)])


def crossed(value, first, by):
    at = lambda y, c, x: ((y // 2 * 2 + c) * 2 + y % 2) * SIDE + x
    pairs = []
    for c in range(2):
        along_x = (c == 0) == first
        for y in range(SIDE):
            for x in range(SIDE):
                to = (y, c, (x + by) % SIDE) if along_x else ((y + by) % SIDE, c, x)
                pairs.append((at(y, c, x), at(*to)))
    return lax.ppermute(value, PLANE, pairs)


def shaped(shape, dtype):
    return jax.ShapeDtypeStruct(shape, dtype)


def local(kernel, outs, *args, scalars=0, out_specs=None, flops=0):
    many = isinstance(outs, list)
    return pl.pallas_call(
        kernel,
        out_shape=outs,
        in_specs=[SMEM] * scalars + [VMEM] * (len(args) - scalars),
        out_specs=out_specs or ([VMEM] * len(outs) if many else VMEM),
        compiler_params=pltpu.CompilerParams(vmem_limit_bytes=16 * 2**20),
        cost_estimate=pl.CostEstimate(
            flops=flops,
            bytes_accessed=sum(a.size * a.dtype.itemsize for a in args),
            transcendentals=0,
        ),
    )(*args)


def matmul(a, b, contract):
    return lax.dot_general(a, b, (contract, ((), ())), preferred_element_type=F32)


def inverse(raw):
    return lax.rsqrt(jnp.sum(raw * raw, axis=1, keepdims=True) + 1e-06)


def normalize_kernel(img_ref, txt_ref, img_out, txt_out):
    for raw, out in ((txt_ref, txt_out), (img_ref, img_out)):
        out[...] = (raw[...] * inverse(raw[...])).astype(BF16)


def join_kernel(*refs):
    *blocks, out_ref = refs
    at = 0
    for block in blocks:
        out_ref[pl.ds(at, block.shape[0]), :] = block[...]
        at += block.shape[0]


def weights_of(images, texts, scale, bias, paired):
    logits = scale * matmul(images, texts, ((1,), (1,))) + bias
    if not paired:
        return (1.0 / (1.0 + jnp.exp(-logits))).astype(BF16)
    img_at = lax.broadcasted_iota(jnp.int32, logits.shape, 0)
    txt_at = lax.broadcasted_iota(jnp.int32, logits.shape, 1)
    sign = jnp.where((img_at == txt_at) & (img_at < paired), 1.0, -1.0).astype(F32)
    return (-sign / (1.0 + jnp.exp(sign * logits))).astype(BF16)


def image_kernel(paired, scale_ref, bias_ref, txt_ref, *refs):
    *blocks, w_ref, d_ref, img_ref = refs
    scale = scale_ref[0]
    for i, block in enumerate(blocks):
        tile = pl.ds(i * block.shape[0], block.shape[0])
        images = block[...]
        img_ref[tile, :] = images
        weights = weights_of(images, txt_ref[...], scale, bias_ref[0], 0 if i else paired)
        w_ref[tile, :] = weights
        d_ref[tile, :] = (scale * matmul(weights, txt_ref[...], ((1,), (0,)))).astype(d_ref.dtype)


def text_kernel(places, scale_ref, w_mine_ref, w_theirs_ref, mine_ref, theirs_ref, *outs):
    for place, out in zip(places, outs):
        cols = pl.ds(place * TILE, TILE)
        total = matmul(w_mine_ref[:, cols], mine_ref[...], ((0,), (0,)))
        total += matmul(w_theirs_ref[:, cols], theirs_ref[...], ((0,), (0,)))
        out[...] = (scale_ref[0] * total).astype(out.dtype)


def split_kernel(count, *refs):
    arrays, outs = (refs[:count], refs[count:])
    rows = outs[0].shape[0]
    for i in reversed(range(len(outs))):
        tile = pl.ds(i * rows, rows)
        total = arrays[0][tile, :].astype(F32)
        for array in arrays[1:]:
            total += array[tile, :].astype(F32)
        outs[i][...] = total.astype(outs[i].dtype)


def add_kernel(a_ref, b_ref, out_ref):
    out_ref[...] = (a_ref[...].astype(F32) + b_ref[...].astype(F32)).astype(BF16)


def end_kernel(raw_ref, *refs):
    *parts, out_ref = refs
    raw, grad = (raw_ref[...], parts[0][...].astype(F32))
    for part in parts[1:]:
        grad += part[...].astype(F32)
    inv = inverse(raw)
    across = jnp.sum(raw * grad, axis=1, keepdims=True)
    out_ref[...] = inv * grad - raw * (inv * inv * inv) * across


def added(a, b):
    return local(add_kernel, shaped(a.shape, BF16), a, b)


def body(images, texts, scale, bias):
    rows, width = images.shape
    line, half, all_txt = (SIDE * rows, 8 * rows, SIDE * SIDE * rows)
    block = shaped((rows, width), BF16)
    join = lambda *parts: local(
        join_kernel, shaped((sum(part.shape[0] for part in parts), width), BF16), *parts
    )
    img, txt = local(normalize_kernel, [block, block], images, texts)

    ahead, behind, across = [crossed(txt, True, by) for by in (1, -1, 2)]
    up1, down1, far = (shifted(img, "z", 1), shifted(img, "z", -1), shifted(img, "z", 4))
    texts0 = join(txt, ahead, behind, across)
    texts1, texts2, texts3 = [crossed(texts0, False, by) for by in (1, -1, 2)]
    up2, down2 = (shifted(up1, "z", 1), shifted(down1, "z", -1))
    mine_a = join(img, up1, down1, far)
    theirs_a = shifted(mine_a, "c", 1)
    up3, down3 = (shifted(up2, "z", 1), shifted(down2, "z", -1))
    mine_b = join(up2, down2, up3, down3)
    theirs_b = shifted(mine_b, "c", 1)
    txt_all = join(texts0, texts1, texts2, texts3)

    flops = 2 * half * all_txt * width
    halves = lambda paired, kind, *parts: local(
        functools.partial(image_kernel, paired),
        [shaped((half, all_txt), BF16), shaped((half, width), kind), shaped((half, width), BF16)],
        scale, bias, txt_all, *parts,
        scalars=2, flops=2 * flops,
    )
    w_mine, d_mine, mine = halves(rows, F32, mine_a, mine_b)
    w_theirs, d_theirs, theirs = halves(0, BF16, theirs_a, theirs_b)
    back = shifted(d_theirs, "c", 1)
    gradients = lambda places, kind: local(
        functools.partial(text_kernel, places),
        [shaped((line, width), kind) for _ in places],
        scale, w_mine, w_theirs, mine, theirs,
        scalars=1, flops=2 * flops * len(places) // SIDE,
    )
    d_texts3, d_texts1, d_texts2 = gradients((3, 1, 2), BF16)
    d_texts0 = gradients((0,), F32)[0]

    back3, back1, back2 = (
        crossed(d_texts3, False, 2),
        crossed(d_texts1, False, -1),
        crossed(d_texts2, False, 1),
    )
    kinds = [F32] + [BF16] * 7
    own, m1, p1, d_far, m2, p2, m3, p3 = local(
        functools.partial(split_kernel, 2),
        [shaped((rows, width), kind) for kind in kinds],
        d_mine, back,
    )
    up, down = (shifted(m3, "z", -1), shifted(p3, "z", 1))
    d_far = shifted(d_far, "z", 4)
    up, down = (shifted(added(m2, up), "z", -1), shifted(added(p2, down), "z", 1))
    up, down = (shifted(added(m1, up), "z", -1), shifted(added(p1, down), "z", 1))
    txt_own, d_ahead, d_behind, d_across = local(
        functools.partial(split_kernel, 4),
        [shaped((rows, width), kind) for kind in kinds[:SIDE]],
        d_texts0, back1, back2, back3,
    )
    d_ahead, d_behind, d_across = (
        crossed(d_ahead, True, -1),
        crossed(d_behind, True, 1),
        crossed(d_across, True, 2),
    )

    whole = pl.BlockSpec((rows, width), lambda: (0, 0))
    end = lambda raw, *parts: local(
        end_kernel, shaped((rows, width), F32), raw, *parts, out_specs=whole
    )
    return (end(images, own, up, down, d_far), end(texts, txt_own, d_ahead, d_behind, d_across))


def solution(mesh):
    fine = Mesh(mesh.devices.reshape(8, 2, 2, 2, 4), AXES)
    rows = P(AXES, None)
    return jax.shard_map(
        body,
        mesh=fine,
        in_specs=(rows, rows, P(), P()),
        out_specs=(rows, rows),
        check_vma=False,
    )
```

```python
import functools

import jax
import jax.numpy as jnp
from jax import lax
from jax.experimental import pallas as pl
from jax.experimental.pallas import tpu as pltpu
from jax.sharding import Mesh, PartitionSpec as P

AXES = ("z", "yh", "c", "yl", "x")
PLANE = ("yh", "c", "yl", "x")
SIDE = 4
BF16 = jnp.bfloat16
F32 = jnp.float32
VMEM = pl.BlockSpec(memory_space=pltpu.VMEM)
HBM = pl.BlockSpec(memory_space=pltpu.HBM)
SMEM = pl.BlockSpec(memory_space=pltpu.SMEM)
TILE = 256


def shifted(value, axis, by):
    length = lax.axis_size(axis)
    return lax.ppermute(value, axis, [(i, (i + by) % length) for i in range(length)])


def crossed(value, first, by):
    at = lambda y, c, x: ((y // 2 * 2 + c) * 2 + y % 2) * SIDE + x
    pairs = []
    for c in range(2):
        along_x = (c == 0) == first
        for y in range(SIDE):
            for x in range(SIDE):
                to = (y, c, (x + by) % SIDE) if along_x else ((y + by) % SIDE, c, x)
                pairs.append((at(y, c, x), at(*to)))
    return lax.ppermute(value, PLANE, pairs)


def fanned(value, by):
    length = lax.axis_size("z")
    pairs = [
        (z * 2 + c, (z + (by if c == 0 else -by)) % length * 2 + c)
        for z in range(length)
        for c in range(2)
    ]
    return lax.ppermute(value, ("z", "c"), pairs)


def shaped(shape, dtype):
    return jax.ShapeDtypeStruct(shape, dtype)


def local(kernel, outs, *args, scalars=0, out_specs=None, flops=0, scratch=(), place=VMEM):
    many = isinstance(outs, list)
    if place is HBM:
        args = [pltpu.with_memory_space_constraint(arg, pltpu.HBM) for arg in args]
    return pl.pallas_call(
        kernel,
        out_shape=outs,
        in_specs=[SMEM] * scalars + [place] * (len(args) - scalars),
        out_specs=out_specs or ([VMEM] * len(outs) if many else VMEM),
        scratch_shapes=list(scratch),
        compiler_params=pltpu.CompilerParams(vmem_limit_bytes=16 * 2**20),
        cost_estimate=pl.CostEstimate(
            flops=flops,
            bytes_accessed=sum(a.size * a.dtype.itemsize for a in args),
            transcendentals=0,
        ),
    )(*args)


def matmul(a, b, contract):
    return lax.dot_general(a, b, (contract, ((), ())), preferred_element_type=F32)


def inverse(raw):
    return lax.rsqrt(jnp.sum(raw * raw, axis=1, keepdims=True) + 1e-06)


def normalize_kernel(img_in, txt_in, img_out, txt_out, raw, sems):
    reads = [pltpu.make_async_copy(a, raw.at[i], sems.at[i]) for i, a in enumerate((txt_in, img_in))]
    for read in reads:
        read.start()
    for i, out in enumerate((txt_out, img_out)):
        reads[i].wait()
        out[...] = (raw[i] * inverse(raw[i])).astype(BF16)


def join_kernel(*refs):
    *blocks, out_ref = refs
    at = 0
    for block in blocks:
        out_ref[pl.ds(at, block.shape[0]), :] = block[...]
        at += block.shape[0]


def weights_of(images, texts, scale, bias, paired):
    logits = scale * matmul(images, texts, ((1,), (1,))) + bias
    if not paired:
        return (1.0 / (1.0 + jnp.exp(-logits))).astype(BF16)
    img_at = lax.broadcasted_iota(jnp.int32, logits.shape, 0)
    txt_at = lax.broadcasted_iota(jnp.int32, logits.shape, 1)
    sign = jnp.where((img_at == txt_at) & (img_at < paired), 1.0, -1.0).astype(F32)
    return (-sign / (1.0 + jnp.exp(sign * logits))).astype(BF16)


def image_kernel(paired, pieces, groups, scale_ref, bias_ref, *refs):
    texts, images = (refs[:pieces], refs[pieces : pieces + groups])
    before = refs[pieces + groups : -2 * groups]
    weights_out, grads_out = (refs[-2 * groups : -groups], refs[-groups:])
    scale = scale_ref[0]
    for i in range(groups):
        total = None
        for j, text in enumerate(texts):
            pair = 0 if i or j else paired
            weights = weights_of(images[i][...], text[...], scale, bias_ref[0], pair)
            weights_out[i][:, pl.ds(j * TILE, TILE)] = weights
            part = matmul(weights, text[...], ((1,), (0,)))
            total = part if total is None else total + part
        total = scale * total
        if before:
            total += before[i][...]
        grads_out[i][...] = total.astype(grads_out[i].dtype)


def text_kernel(places, scale_ref, *refs):
    images, weights, outs = (refs[:4], refs[4 : -len(places)], refs[-len(places) :])
    for place, out in zip(places, outs):
        total = None
        for image, (array, at) in zip(images, place):
            w = weights[array][:, pl.ds(at * TILE, TILE)]
            part = matmul(w, image[...], ((0,), (0,)))
            total = part if total is None else total + part
        out[...] = (scale_ref[0] * total).astype(out.dtype)


def split_kernel(count, *refs):
    arrays, outs = (refs[:count], refs[count:])
    at = 0
    for out in outs:
        tile = pl.ds(at, out.shape[0])
        total = arrays[0][tile, :].astype(F32)
        for array in arrays[1:]:
            total += array[tile, :].astype(F32)
        out[...] = total.astype(out.dtype)
        at += out.shape[0]


def add_kernel(a_ref, b_ref, out_ref):
    out_ref[...] = (a_ref[...].astype(F32) + b_ref[...].astype(F32)).astype(BF16)


def ring_add_kernel(own_ref, sib_ref, far_ref, out_ref):
    rows = own_ref.shape[0]
    total = own_ref[...].astype(F32) + far_ref[...].astype(F32)
    out_ref[pl.ds(0, rows), :] = total.astype(BF16)
    out_ref[pl.ds(rows, rows), :] = sib_ref[...]


def end_kernel(raw_ref, *refs):
    *parts, out_ref = refs
    raw, grad = (raw_ref[...], parts[0][...].astype(F32))
    for part in parts[1:]:
        grad += part[...].astype(F32)
    inv = inverse(raw)
    across = jnp.sum(raw * grad, axis=1, keepdims=True)
    out_ref[...] = inv * grad - raw * (inv * inv * inv) * across


def added(a, b):
    return local(add_kernel, shaped(a.shape, BF16), a, b)


def body(images, texts, scale, bias):
    rows, width = images.shape
    line, half = (SIDE * rows, 8 * rows)
    block = shaped((rows, width), BF16)
    join = lambda *parts: local(
        join_kernel, shaped((sum(part.shape[0] for part in parts), width), BF16), *parts
    )
    img, txt = local(
        normalize_kernel,
        [block, block],
        images, texts,
        place=HBM,
        scratch=[pltpu.VMEM((2, rows, width), F32), pltpu.SemaphoreType.DMA((2,))],
    )

    def image_part(paired, pieces, groups, before, kinds):
        size = groups[0].shape[0]
        outs = [shaped((size, len(pieces) * line), BF16) for _ in groups]
        results = local(
            functools.partial(image_kernel, paired, len(pieces), len(groups)),
            outs + [shaped((size, width), kind) for kind in kinds],
            scale, bias, *pieces, *groups, *before,
            scalars=2, flops=4 * size * len(groups) * line * len(pieces) * width,
        )
        return results[: len(groups)], results[len(groups) :]

    ahead, behind, across = [crossed(txt, True, by) for by in (1, -1, 2)]
    texts0 = join(txt, ahead, behind, across)
    sib = shifted(img, "c", 1)
    keep_1 = join(img, sib)
    z1 = fanned(keep_1, 1)
    texts0, z1 = lax.optimization_barrier((texts0, z1))
    texts1, texts2, texts3 = [crossed(texts0, False, by) for by in (1, -1, 2)]
    others = (texts3, texts1, texts2)
    z1_sib = shifted(z1, "c", 1)
    z2 = fanned(z1, 1)
    z2, z1_sib = lax.optimization_barrier((z2, z1_sib))
    keep_a, send_a = (join(img, z1), join(sib, z1_sib))
    w_a0, d_a0 = image_part(rows, (texts0,), (keep_a, send_a), (), (F32, F32))
    z3 = fanned(z2, 1)
    z3, *d_a0 = lax.optimization_barrier((z3, *d_a0))
    far = fanned(z3[:rows], 1)
    w_a, (dk_a, ds_a) = image_part(0, others, (keep_a, send_a), d_a0, (F32, BF16))
    far, ds_a = lax.optimization_barrier((far, ds_a))
    keep_b = join(z2, z3, far)
    send_b = shifted(keep_b, "c", 1)

    w_sb, (ds_b,) = image_part(0, (texts0, *others), (send_b,), (), (BF16,))
    back_b, back_a = (shifted(ds_b, "c", 1), shifted(ds_a, "c", 1))
    w_kb, (dk_b,) = image_part(0, (texts0, *others), (keep_b,), (), (F32,))

    def text_part(places, kind):
        return local(
            functools.partial(text_kernel, places),
            [shaped((line, width), kind) for _ in places],
            scale, keep_a, send_a, send_b, keep_b, *w_a0, *w_a, *w_sb, *w_kb,
            scalars=1, flops=2 * len(places) * line * 16 * rows * width,
        )

    d_texts3, d_texts1, d_texts2 = text_part(
        [[(2, i), (3, i), (4, i + 1), (5, i + 1)] for i in range(3)], BF16
    )
    d_texts0 = text_part([[(0, 0), (1, 0), (4, 0), (5, 0)]], F32)[0]

    z2_sum, z3_own, z3_sib, far_sum = local(
        functools.partial(split_kernel, 2),
        [shaped((2 * rows, width), BF16), block, block, block],
        dk_b, back_b,
    )
    own, z1_sum = local(
        functools.partial(split_kernel, 2),
        [shaped((rows, width), F32), shaped((2 * rows, width), BF16)],
        dk_a, back_a,
    )
    far_back = fanned(far_sum, -1)
    far_back, d_texts3, d_texts1, d_texts2 = lax.optimization_barrier((far_back, d_texts3, d_texts1, d_texts2))
    back3, back1, back2 = (
        crossed(d_texts3, False, 2),
        crossed(d_texts1, False, -1),
        crossed(d_texts2, False, 1),
    )
    kinds = [F32] + [BF16] * 3
    returned = local(
        ring_add_kernel, shaped((2 * rows, width), BF16), z3_own, z3_sib, far_back
    )
    returned = fanned(returned, -1)
    returned = fanned(added(z2_sum, returned), -1)
    returned = fanned(added(z1_sum, returned), -1)
    other = shifted(returned[rows:], "c", 1)
    txt_own, d_ahead, d_behind, d_across = local(
        functools.partial(split_kernel, 4),
        [shaped((rows, width), kind) for kind in kinds],
        d_texts0, back1, back2, back3,
    )
    d_ahead, d_behind, d_across = (
        crossed(d_ahead, True, -1),
        crossed(d_behind, True, 1),
        crossed(d_across, True, 2),
    )

    whole = pl.BlockSpec((rows, width), lambda: (0, 0))
    end = lambda raw, *parts: local(
        end_kernel, shaped((rows, width), F32), raw, *parts, out_specs=whole
    )
    return (end(images, own, returned[:rows], other), end(texts, txt_own, d_ahead, d_behind, d_across))


def solution(mesh):
    fine = Mesh(mesh.devices.reshape(8, 2, 2, 2, 4), AXES)
    rows = P(AXES, None)
    return jax.shard_map(
        body,
        mesh=fine,
        in_specs=(rows, rows, P(), P()),
        out_specs=(rows, rows),
        check_vma=False,
    )
```

```python
import functools

import jax
import jax.numpy as jnp
from jax import lax
from jax.experimental import pallas as pl
from jax.experimental.pallas import tpu as pltpu
from jax.sharding import Mesh, PartitionSpec as P

AXES = ("z", "yh", "c", "yl", "x")
PLANE = ("yh", "c", "yl", "x")
SIDE = 4
BF16 = jnp.bfloat16
F32 = jnp.float32
VMEM = pl.BlockSpec(memory_space=pltpu.VMEM)
HBM = pl.BlockSpec(memory_space=pltpu.HBM)
SMEM = pl.BlockSpec(memory_space=pltpu.SMEM)
TILE = 256


def shifted(value, axis, by):
    length = lax.axis_size(axis)
    return lax.ppermute(value, axis, [(i, (i + by) % length) for i in range(length)])


def crossed(value, first, by):
    at = lambda y, c, x: ((y // 2 * 2 + c) * 2 + y % 2) * SIDE + x
    pairs = []
    for c in range(2):
        along_x = (c == 0) == first
        for y in range(SIDE):
            for x in range(SIDE):
                to = (y, c, (x + by) % SIDE) if along_x else ((y + by) % SIDE, c, x)
                pairs.append((at(y, c, x), at(*to)))
    return lax.ppermute(value, PLANE, pairs)


def fanned(value, by):
    length = lax.axis_size("z")
    pairs = [
        (z * 2 + c, (z + (by if c == 0 else -by)) % length * 2 + c)
        for z in range(length)
        for c in range(2)
    ]
    return lax.ppermute(value, ("z", "c"), pairs)


def shaped(shape, dtype):
    return jax.ShapeDtypeStruct(shape, dtype)


def local(kernel, outs, *args, scalars=0, out_specs=None, flops=0, scratch=(), place=VMEM):
    many = isinstance(outs, list)
    if place is HBM:
        args = [pltpu.with_memory_space_constraint(arg, pltpu.HBM) for arg in args]
    return pl.pallas_call(
        kernel,
        out_shape=outs,
        in_specs=[SMEM] * scalars + [place] * (len(args) - scalars),
        out_specs=out_specs or ([VMEM] * len(outs) if many else VMEM),
        scratch_shapes=list(scratch),
        compiler_params=pltpu.CompilerParams(vmem_limit_bytes=16 * 2**20),
        cost_estimate=pl.CostEstimate(
            flops=flops,
            bytes_accessed=sum(a.size * a.dtype.itemsize for a in args),
            transcendentals=0,
        ),
    )(*args)


def matmul(a, b, contract):
    return lax.dot_general(a, b, (contract, ((), ())), preferred_element_type=F32)


def inverse(raw):
    return lax.rsqrt(jnp.sum(raw * raw, axis=1, keepdims=True) + 1e-06)


def normalize_kernel(img_in, txt_in, img_out, txt_out, raw, sems):
    reads = [pltpu.make_async_copy(a, raw.at[i], sems.at[i]) for i, a in enumerate((txt_in, img_in))]
    for read in reads:
        read.start()
    for i, out in enumerate((txt_out, img_out)):
        reads[i].wait()
        out[...] = (raw[i] * inverse(raw[i])).astype(BF16)


def join_kernel(*refs):
    *blocks, out_ref = refs
    at = 0
    for block in blocks:
        out_ref[pl.ds(at, block.shape[0]), :] = block[...]
        at += block.shape[0]


def weights_of(images, texts, scale, bias, paired):
    logits = scale * matmul(images, texts, ((1,), (1,))) + bias
    if not paired:
        return (1.0 / (1.0 + jnp.exp(-logits))).astype(BF16)
    img_at = lax.broadcasted_iota(jnp.int32, logits.shape, 0)
    txt_at = lax.broadcasted_iota(jnp.int32, logits.shape, 1)
    sign = jnp.where((img_at == txt_at) & (img_at < paired), 1.0, -1.0).astype(F32)
    return (-sign / (1.0 + jnp.exp(sign * logits))).astype(BF16)


def image_kernel(paired, pieces, groups, scale_ref, bias_ref, *refs):
    texts, images = (refs[:pieces], refs[pieces : pieces + groups])
    before = refs[pieces + groups : -2 * groups]
    weights_out, grads_out = (refs[-2 * groups : -groups], refs[-groups:])
    scale = scale_ref[0]
    for i in range(groups):
        total = None
        for j, text in enumerate(texts):
            pair = 0 if i or j else paired
            weights = weights_of(images[i][...], text[...], scale, bias_ref[0], pair)
            weights_out[i][:, pl.ds(j * TILE, TILE)] = weights
            part = matmul(weights, text[...], ((1,), (0,)))
            total = part if total is None else total + part
        total = scale * total
        if before:
            total += before[i][...]
        grads_out[i][...] = total.astype(grads_out[i].dtype)


def text_kernel(places, scale_ref, *refs):
    images, weights, outs = (refs[:4], refs[4 : -len(places)], refs[-len(places) :])
    for place, out in zip(places, outs):
        total = None
        for image, (array, at) in zip(images, place):
            w = weights[array][:, pl.ds(at * TILE, TILE)]
            part = matmul(w, image[...], ((0,), (0,)))
            total = part if total is None else total + part
        out[...] = (scale_ref[0] * total).astype(out.dtype)


def split_kernel(count, *refs):
    arrays, outs = (refs[:count], refs[count:])
    at = 0
    for out in outs:
        tile = pl.ds(at, out.shape[0])
        total = arrays[0][tile, :].astype(F32)
        for array in arrays[1:]:
            total += array[tile, :].astype(F32)
        out[...] = total.astype(out.dtype)
        at += out.shape[0]


def add_kernel(a_ref, b_ref, out_ref):
    out_ref[...] = (a_ref[...].astype(F32) + b_ref[...].astype(F32)).astype(BF16)


def ring_add_kernel(own_ref, sib_ref, far_ref, out_ref):
    rows = own_ref.shape[0]
    total = own_ref[...].astype(F32) + far_ref[...].astype(F32)
    out_ref[pl.ds(0, rows), :] = total.astype(BF16)
    out_ref[pl.ds(rows, rows), :] = sib_ref[...]


def gradient_of(raw, parts):
    grad = parts[0][...].astype(F32)
    for part in parts[1:]:
        grad += part[...].astype(F32)
    inv = inverse(raw)
    across = jnp.sum(raw * grad, axis=1, keepdims=True)
    return inv * grad - raw * (inv * inv * inv) * across


def end_kernel(count, img_ref, txt_ref, *refs):
    *parts, img_out, txt_out = refs
    img_out[...] = gradient_of(img_ref[...], parts[:count])
    txt_out[...] = gradient_of(txt_ref[...], parts[count:])


def added(a, b):
    return local(add_kernel, shaped(a.shape, BF16), a, b)


def body(images, texts, scale, bias):
    rows, width = images.shape
    line, half = (SIDE * rows, 8 * rows)
    block = shaped((rows, width), BF16)
    join = lambda *parts: local(
        join_kernel, shaped((sum(part.shape[0] for part in parts), width), BF16), *parts
    )
    img, txt = local(
        normalize_kernel,
        [block, block],
        images, texts,
        place=HBM,
        scratch=[pltpu.VMEM((2, rows, width), F32), pltpu.SemaphoreType.DMA((2,))],
    )

    def image_part(paired, pieces, groups, before, kinds):
        size = groups[0].shape[0]
        outs = [shaped((size, len(pieces) * line), BF16) for _ in groups]
        results = local(
            functools.partial(image_kernel, paired, len(pieces), len(groups)),
            outs + [shaped((size, width), kind) for kind in kinds],
            scale, bias, *pieces, *groups, *before,
            scalars=2, flops=4 * size * len(groups) * line * len(pieces) * width,
        )
        return results[: len(groups)], results[len(groups) :]

    ahead, behind, across = [crossed(txt, True, by) for by in (1, -1, 2)]
    texts0 = join(txt, ahead, behind, across)
    sib = shifted(img, "c", 1)
    keep_1 = join(img, sib)
    z1 = fanned(keep_1, 1)
    texts0, z1 = lax.optimization_barrier((texts0, z1))
    texts1, texts2, texts3 = [crossed(texts0, False, by) for by in (1, -1, 2)]
    others = (texts3, texts1, texts2)
    z1_sib = shifted(z1, "c", 1)
    z2 = fanned(z1, 1)
    keep_a, send_a = (join(img, z1, z2), join(sib, z1_sib, shifted(z2, "c", 1)))
    w_a0, d_a0 = image_part(rows, (texts0,), (keep_a, send_a), (), (F32, F32))
    z3 = fanned(z2, 1)
    z3, *d_a0 = lax.optimization_barrier((z3, *d_a0))
    far = fanned(z3[:rows], 1)
    far, *others = lax.optimization_barrier((far, *others))
    keep_b = join(z3, far)
    send_b = shifted(keep_b, "c", 1)
    w_a, (dk_a, ds_a) = image_part(0, others, (keep_a, send_a), d_a0, (F32, BF16))
    send_b, ds_a = lax.optimization_barrier((send_b, ds_a))

    w_sb, (ds_b,) = image_part(0, (texts0, *others), (send_b,), (), (BF16,))
    back_b, back_a = (shifted(ds_b, "c", 1), shifted(ds_a, "c", 1))
    w_kb, (dk_b,) = image_part(0, (texts0, *others), (keep_b,), (), (F32,))

    def text_part(places, kind):
        return local(
            functools.partial(text_kernel, places),
            [shaped((line, width), kind) for _ in places],
            scale, keep_a, send_a, send_b, keep_b, *w_a0, *w_a, *w_sb, *w_kb,
            scalars=1, flops=2 * len(places) * line * 16 * rows * width,
        )

    d_texts3, d_texts1, d_texts2 = text_part(
        [[(2, i), (3, i), (4, i + 1), (5, i + 1)] for i in range(3)], BF16
    )
    d_texts0 = text_part([[(0, 0), (1, 0), (4, 0), (5, 0)]], F32)[0]

    z3_own, z3_sib, far_sum = local(
        functools.partial(split_kernel, 2), [block] * 3, dk_b, back_b
    )
    own, z1_sum, z2_sum = local(
        functools.partial(split_kernel, 2),
        [shaped((rows, width), F32)] + [shaped((2 * rows, width), BF16)] * 2,
        dk_a, back_a,
    )
    far_back = fanned(far_sum, -1)
    far_back, d_texts3, d_texts1, d_texts2 = lax.optimization_barrier((far_back, d_texts3, d_texts1, d_texts2))
    back3, back1, back2 = (
        crossed(d_texts3, False, 2),
        crossed(d_texts1, False, -1),
        crossed(d_texts2, False, 1),
    )
    kinds = [F32] + [BF16] * 3
    returned = local(
        ring_add_kernel, shaped((2 * rows, width), BF16), z3_own, z3_sib, far_back
    )
    returned = fanned(returned, -1)
    returned = fanned(added(z2_sum, returned), -1)
    returned, back3 = lax.optimization_barrier((returned, back3))
    returned = fanned(added(z1_sum, returned), -1)
    other = shifted(returned[rows:], "c", 1)
    txt_own, d_ahead, d_behind, d_across = local(
        functools.partial(split_kernel, 4),
        [shaped((rows, width), kind) for kind in kinds],
        d_texts0, back1, back2, back3,
    )
    d_ahead, d_behind, d_across = (
        crossed(d_ahead, True, -1),
        crossed(d_behind, True, 1),
        crossed(d_across, True, 2),
    )

    whole = pl.BlockSpec((rows, width), lambda: (0, 0))
    img_parts = (own, returned[:rows], other)
    return local(
        functools.partial(end_kernel, len(img_parts)),
        [shaped((rows, width), F32)] * 2,
        images, texts, *img_parts, txt_own, d_ahead, d_behind, d_across,
        out_specs=[whole, whole],
    )


def solution(mesh):
    fine = Mesh(mesh.devices.reshape(8, 2, 2, 2, 4), AXES)
    rows = P(AXES, None)
    return jax.shard_map(
        body,
        mesh=fine,
        in_specs=(rows, rows, P(), P()),
        out_specs=(rows, rows),
        check_vma=False,
    )
```

```python
import functools

import jax
import jax.numpy as jnp
from jax import lax
from jax.experimental import pallas as pl
from jax.experimental.pallas import tpu as pltpu
from jax.sharding import Mesh, PartitionSpec as P

AXES = ("z", "yh", "c", "yl", "x")
PLANE = ("yh", "c", "yl", "x")
SIDE = 4
BF16 = jnp.bfloat16
F32 = jnp.float32
VMEM = pl.BlockSpec(memory_space=pltpu.VMEM)
HBM = pl.BlockSpec(memory_space=pltpu.HBM)
SMEM = pl.BlockSpec(memory_space=pltpu.SMEM)
TILE = 256


def shifted(value, axis, by):
    length = lax.axis_size(axis)
    return lax.ppermute(value, axis, [(i, (i + by) % length) for i in range(length)])


def crossed(value, first, by):
    at = lambda y, c, x: ((y // 2 * 2 + c) * 2 + y % 2) * SIDE + x
    pairs = []
    for c in range(2):
        along_x = (c == 0) == first
        for y in range(SIDE):
            for x in range(SIDE):
                to = (y, c, (x + by) % SIDE) if along_x else ((y + by) % SIDE, c, x)
                pairs.append((at(y, c, x), at(*to)))
    return lax.ppermute(value, PLANE, pairs)


def fanned(value, by):
    length = lax.axis_size("z")
    pairs = [
        (z * 2 + c, (z + (by if c == 0 else -by)) % length * 2 + c)
        for z in range(length)
        for c in range(2)
    ]
    return lax.ppermute(value, ("z", "c"), pairs)


def shaped(shape, dtype):
    return jax.ShapeDtypeStruct(shape, dtype)


def local(kernel, outs, *args, scalars=0, out_specs=None, flops=0, scratch=(), place=VMEM):
    many = isinstance(outs, list)
    if place is HBM:
        args = [pltpu.with_memory_space_constraint(arg, pltpu.HBM) for arg in args]
    return pl.pallas_call(
        kernel,
        out_shape=outs,
        in_specs=[SMEM] * scalars + [place] * (len(args) - scalars),
        out_specs=out_specs or ([VMEM] * len(outs) if many else VMEM),
        scratch_shapes=list(scratch),
        compiler_params=pltpu.CompilerParams(vmem_limit_bytes=16 * 2**20),
        cost_estimate=pl.CostEstimate(
            flops=flops,
            bytes_accessed=sum(a.size * a.dtype.itemsize for a in args),
            transcendentals=0,
        ),
    )(*args)


def matmul(a, b, contract):
    return lax.dot_general(a, b, (contract, ((), ())), preferred_element_type=F32)


def inverse(raw):
    return lax.rsqrt(jnp.sum(raw * raw, axis=1, keepdims=True) + 1e-06)


def normalize_kernel(img_in, txt_in, img_out, txt_out, raw, sems):
    reads = [pltpu.make_async_copy(a, raw.at[i], sems.at[i]) for i, a in enumerate((txt_in, img_in))]
    for read in reads:
        read.start()
    for i, out in enumerate((txt_out, img_out)):
        reads[i].wait()
        out[...] = (raw[i] * inverse(raw[i])).astype(BF16)


def join_kernel(*refs):
    *blocks, out_ref = refs
    at = 0
    for block in blocks:
        out_ref[pl.ds(at, block.shape[0]), :] = block[...]
        at += block.shape[0]


def weights_of(images, texts, scale, bias, paired):
    logits = scale * matmul(images, texts, ((1,), (1,))) + bias
    if not paired:
        return (1.0 / (1.0 + jnp.exp(-logits))).astype(BF16)
    img_at = lax.broadcasted_iota(jnp.int32, logits.shape, 0)
    txt_at = lax.broadcasted_iota(jnp.int32, logits.shape, 1)
    sign = jnp.where((img_at == txt_at) & (img_at < paired), 1.0, -1.0).astype(F32)
    return (-sign / (1.0 + jnp.exp(sign * logits))).astype(BF16)


def image_kernel(paired, pieces, groups, scale_ref, bias_ref, *refs):
    texts, images = (refs[:pieces], refs[pieces : pieces + groups])
    before = refs[pieces + groups : -2 * groups]
    weights_out, grads_out = (refs[-2 * groups : -groups], refs[-groups:])
    scale = scale_ref[0]
    for i in range(groups):
        total = None
        for j, text in enumerate(texts):
            pair = 0 if i or j else paired
            weights = weights_of(images[i][...], text[...], scale, bias_ref[0], pair)
            weights_out[i][:, pl.ds(j * TILE, TILE)] = weights
            part = matmul(weights, text[...], ((1,), (0,)))
            total = part if total is None else total + part
        total = scale * total
        if before:
            total += before[i][...]
        grads_out[i][...] = total.astype(grads_out[i].dtype)


def text_kernel(places, scale_ref, *refs):
    images, weights, outs = (refs[:4], refs[4 : -len(places)], refs[-len(places) :])
    for place, out in zip(places, outs):
        total = None
        for image, (array, at) in zip(images, place):
            w = weights[array][:, pl.ds(at * TILE, TILE)]
            part = matmul(w, image[...], ((0,), (0,)))
            total = part if total is None else total + part
        out[...] = (scale_ref[0] * total).astype(out.dtype)


def split_kernel(count, *refs):
    arrays, outs = (refs[:count], refs[count:])
    at = 0
    for out in outs:
        tile = pl.ds(at, out.shape[0])
        total = arrays[0][tile, :].astype(F32)
        for array in arrays[1:]:
            total += array[tile, :].astype(F32)
        out[...] = total.astype(out.dtype)
        at += out.shape[0]


def add_kernel(a_ref, b_ref, out_ref):
    out_ref[...] = (a_ref[...].astype(F32) + b_ref[...].astype(F32)).astype(BF16)


def ring_add_kernel(own_ref, sib_ref, far_ref, out_ref):
    rows = own_ref.shape[0]
    total = own_ref[...].astype(F32) + far_ref[...].astype(F32)
    out_ref[pl.ds(0, rows), :] = total.astype(BF16)
    out_ref[pl.ds(rows, rows), :] = sib_ref[...]


def gradient_of(raw, parts):
    grad = parts[0][...].astype(F32)
    for part in parts[1:]:
        grad += part[...].astype(F32)
    inv = inverse(raw)
    across = jnp.sum(raw * grad, axis=1, keepdims=True)
    return inv * grad - raw * (inv * inv * inv) * across


def end_kernel(count, img_ref, txt_ref, *refs):
    *parts, img_out, txt_out = refs
    img_out[...] = gradient_of(img_ref[...], parts[:count])
    txt_out[...] = gradient_of(txt_ref[...], parts[count:])


def added(a, b):
    return local(add_kernel, shaped(a.shape, BF16), a, b)


def body(images, texts, scale, bias):
    rows, width = images.shape
    line, half = (SIDE * rows, 8 * rows)
    block = shaped((rows, width), BF16)
    join = lambda *parts: local(
        join_kernel, shaped((sum(part.shape[0] for part in parts), width), BF16), *parts
    )
    img, txt = local(
        normalize_kernel,
        [block, block],
        images, texts,
        place=HBM,
        scratch=[pltpu.VMEM((2, rows, width), F32), pltpu.SemaphoreType.DMA((2,))],
    )

    def image_part(paired, pieces, groups, before, kinds):
        size = groups[0].shape[0]
        outs = [shaped((size, len(pieces) * line), BF16) for _ in groups]
        results = local(
            functools.partial(image_kernel, paired, len(pieces), len(groups)),
            outs + [shaped((size, width), kind) for kind in kinds],
            scale, bias, *pieces, *groups, *before,
            scalars=2, flops=4 * size * len(groups) * line * len(pieces) * width,
        )
        return results[: len(groups)], results[len(groups) :]

    ahead, behind, across = [crossed(txt, True, by) for by in (1, -1, 2)]
    texts0 = join(txt, ahead, behind, across)
    sib = shifted(img, "c", 1)
    keep_1 = join(img, sib)
    z1 = fanned(keep_1, 1)
    texts0, z1 = lax.optimization_barrier((texts0, z1))
    texts1, texts2, texts3 = [crossed(texts0, False, by) for by in (1, -1, 2)]
    others = (texts3, texts1, texts2)
    z1_sib = shifted(z1, "c", 1)
    z2 = fanned(z1, 1)
    keep_a, send_a = (join(img, z1, z2), join(sib, z1_sib, shifted(z2, "c", 1)))
    w_a0, d_a0 = image_part(rows, (texts0,), (keep_a, send_a), (), (F32, F32))
    z3 = fanned(z2, 1)
    z3, *d_a0 = lax.optimization_barrier((z3, *d_a0))
    far = fanned(z3[:rows], 1)
    far, *others = lax.optimization_barrier((far, *others))
    keep_b = join(z3, far)
    send_b = shifted(keep_b, "c", 1)
    w_a, (dk_a, ds_a) = image_part(0, others, (keep_a, send_a), d_a0, (F32, BF16))
    send_b, ds_a = lax.optimization_barrier((send_b, ds_a))

    w_sb, (ds_b,) = image_part(0, (texts0, *others), (send_b,), (), (BF16,))
    back_b, back_a = (shifted(ds_b, "c", 1), shifted(ds_a, "c", 1))
    w_kb, (dk_b,) = image_part(0, (texts0, *others), (keep_b,), (), (F32,))

    def text_part(places, kind):
        return local(
            functools.partial(text_kernel, places),
            [shaped((line, width), kind) for _ in places],
            scale, keep_a, send_a, send_b, keep_b, *w_a0, *w_a, *w_sb, *w_kb,
            scalars=1, flops=2 * len(places) * line * 16 * rows * width,
        )

    d_texts3, d_texts1, d_texts2 = text_part(
        [[(2, i), (3, i), (4, i + 1), (5, i + 1)] for i in range(3)], BF16
    )
    d_texts0 = text_part([[(0, 0), (1, 0), (4, 0), (5, 0)]], F32)[0]

    z3_own, z3_sib, far_sum = local(
        functools.partial(split_kernel, 2), [block] * 3, dk_b, back_b
    )
    own, z1_sum, z2_sum = local(
        functools.partial(split_kernel, 2),
        [shaped((rows, width), F32)] + [shaped((2 * rows, width), BF16)] * 2,
        dk_a, back_a,
    )
    far_back = fanned(far_sum, -1)
    far_back, *_ = lax.optimization_barrier((far_back, d_texts3, d_texts1, d_texts2))
    back3, back1, back2 = (
        crossed(d_texts3, False, 2),
        crossed(d_texts1, False, -1),
        crossed(d_texts2, False, 1),
    )
    kinds = [F32] + [BF16] * 3
    returned = local(
        ring_add_kernel, shaped((2 * rows, width), BF16), z3_own, z3_sib, far_back
    )
    returned = fanned(returned, -1)
    returned = fanned(added(z2_sum, returned), -1)
    returned, back3, d_texts0 = lax.optimization_barrier((returned, back3, d_texts0))
    returned = fanned(added(z1_sum, returned), -1)
    other = shifted(returned[rows:], "c", 1)
    txt_own, d_ahead, d_behind, d_across = local(
        functools.partial(split_kernel, 4),
        [shaped((rows, width), kind) for kind in kinds],
        d_texts0, back1, back2, back3,
    )
    d_ahead, d_behind, d_across = (
        crossed(d_ahead, True, -1),
        crossed(d_behind, True, 1),
        crossed(d_across, True, 2),
    )

    whole = pl.BlockSpec((rows, width), lambda: (0, 0))
    img_parts = (own, returned[:rows], other)
    return local(
        functools.partial(end_kernel, len(img_parts)),
        [shaped((rows, width), F32)] * 2,
        images, texts, *img_parts, txt_own, d_ahead, d_behind, d_across,
        out_specs=[whole, whole],
    )


def solution(mesh):
    fine = Mesh(mesh.devices.reshape(8, 2, 2, 2, 4), AXES)
    rows = P(AXES, None)
    return jax.shard_map(
        body,
        mesh=fine,
        in_specs=(rows, rows, P(), P()),
        out_specs=(rows, rows),
        check_vma=False,
    )
```
